256 devices in a mesh: tm: 64 (over x, z, y_hi), rec: 4 (over y_lo, core).
Axes of the slice: x: 4, y: 4 (y_hi: 2, y_lo: 2; y = y_hi * 2 + y_lo), z: 8, core: 2. Of those that a mesh axis runs over, the one named last changes fastest.
Arguments:
- frames: bfloat16 [12, 8192, 1536], P('rec', 'tm'), parts along dimension 0, may hold values from -6 to 6
- time_starts: int32 [12, 2], P('rec'), parts along dimension 0, may hold values from 0 to 8191
- time_widths: int32 [12, 2], P('rec'), parts along dimension 0, may hold values from 0 to 40
- freq_starts: int32 [12, 2], P('rec'), parts along dimension 0, may hold values from 0 to 1535
- freq_widths: int32 [12, 2], P('rec'), parts along dimension 0, may hold values from 0 to 192
- lengths: int32 [12], P('rec'), parts along dimension 0, may hold values from 4096 to 8192, as said below
- w_query: bfloat16 [1536, 768], replicated, may hold values from -4 to 4
- w_key: bfloat16 [1536, 768], replicated, may hold values from -4 to 4
- w_value: bfloat16 [1536, 768], replicated, may hold values from -0.15625 to 0.15625
- w_out: bfloat16 [768, 1536], replicated, may hold values from -0.21875 to 0.21875
- attn_gain: float32 [1536], replicated, may hold values from 0.1 to 1.9
- conv_gain: float32 [1536], replicated, may hold values from 0.1 to 1.9
- conv_kernel: float32 [31, 1536], replicated, may hold values from -2 to 2
- conv_scale: float32 [1536], replicated, may hold values from 0.3 to 3
Outputs:
- layer_out: bfloat16 [12, 8192, 1536], P('rec', 'tm'), parts along dimension 0
The draws below stay inside these ranges and needn't reach their ends.
There are 4 independent parts, one for each index of `rec`. The reference program is written for one: setup_inputs(seed, part) draws one part's arguments, and reference() takes and returns one part's arrays. A program takes and returns all parts, laid end to end along the dimension named above; an argument that names none is the same for every part. Nothing has to cross between parts.
Inputs may be any that keep to these rules, and one draw needn't show every extreme that they name: `lengths`: at least half of each recording is valid; in every part one recording is valid to its end and one has exactly 4096 valid frames.
All inputs are finite; a program needn't handle non-finite values.
Results may differ from the reference program's by a relative error of at most 0.0065.
Values may be sent and summed in bfloat16 or wider, within the bound.
A program may use at most 64 MiB of HBM per device.

```python
import math
import jax
import jax.numpy as jnp
from jax import lax

D = 1536
HEADS = 12
HSIZE = 64
FRAMES = 128
RECS = 3
KSIZE = 31
MT = 2
MF = 2
TMAX = 40
FMAX = 192
TIME = 8192
HALF = 15


def draw_w_query(key, part):
    key = jax.random.fold_in(key, 11)
    own = jax.random.truncated_normal(key, -4.0, 4.0, (D, HEADS * HSIZE), jnp.float32)
    values = own * D ** (-0.5)
    return values.astype(jnp.bfloat16)


def draw_w_key(key, part):
    key = jax.random.fold_in(key, 13)
    own = jax.random.truncated_normal(key, -4.0, 4.0, (D, HEADS * HSIZE), jnp.float32)
    values = own * D ** (-0.5)
    return values.astype(jnp.bfloat16)


def draw_lengths(key, part):
    key = jax.random.fold_in(key, 17)
    first, second = jax.random.split(key)
    drops = jax.random.randint(first, (RECS,), 0, TIME // 2 + 1, jnp.int32)
    result = TIME - drops
    order = jax.random.permutation(second, RECS)
    result = result.at[order[0]].set(TIME)
    result = result.at[order[1]].set(TIME - TIME // 2)
    return result.astype(jnp.int32)


def touch_ends(values, stream_key, least, high):
    extent = values.shape
    index_at = [jax.random.randint(jax.random.fold_in(stream_key, axis), (), 0, extent[axis]) for axis in range(len(extent))]
    values = values.at[tuple(index_at)].set(least)
    longest = extent.index(max(extent))
    index_at[longest] = (index_at[longest] + 1) % extent[longest]
    return values.at[tuple(index_at)].set(high)


def block_levels(stream_key, extent, shards, least, top_value):
    def one(position, blocks):
        heights = jax.random.uniform(jax.random.fold_in(jax.random.fold_in(stream_key, 6), position), (blocks,), jnp.float32, least / len(shards), top_value / len(shards))
        return jnp.repeat(jnp.exp(heights), extent[position] // blocks).reshape((-1,) + (1,) * (len(extent) - position - 1))

    factor_of = one(*shards[0])
    for cut in shards[1:]:
        factor_of = factor_of * one(*cut)
    return factor_of


def scatter_about(own_key, extent, scale, bound, cuts=(), held_as=jnp.bfloat16):
    drawn = scale * jax.random.normal(own_key, extent, jnp.float32)
    if cuts:
        drawn = drawn * block_levels(own_key, extent, cuts, -0.22, 0.18)
    return jnp.clip(drawn, -bound, bound).astype(held_as)


def setup_inputs(seed: int = 0, part: int = 0) -> dict:
    key_of = jax.random.split(jax.random.key(seed), 15)
    part_keys = jax.random.split(jax.random.fold_in(key_of[14], part), 15)
    frames = scatter_about(part_keys[0], (RECS, TIME, D), 1.0, 6.0, ((1, 64),))
    time_starts = touch_ends(jax.random.randint(part_keys[1], (RECS, MT), 0, TIME), jax.random.fold_in(part_keys[1], 1), 0, TIME - 1).astype(jnp.int32)
    time_widths = touch_ends(jax.random.randint(part_keys[2], (RECS, MT), 0, TMAX + 1), jax.random.fold_in(part_keys[2], 1), 0, TMAX).astype(jnp.int32)
    freq_starts = touch_ends(jax.random.randint(part_keys[3], (RECS, MF), 0, D), jax.random.fold_in(part_keys[3], 1), 0, D - 1).astype(jnp.int32)
    freq_widths = touch_ends(jax.random.randint(part_keys[4], (RECS, MF), 0, FMAX + 1), jax.random.fold_in(part_keys[4], 1), 0, FMAX).astype(jnp.int32)
    lengths = draw_lengths(jax.random.fold_in(jax.random.fold_in(key_of[14], part), 71), part)
    w_query = draw_w_query(jax.random.fold_in(key_of[14], 71), part)
    w_key = draw_w_key(jax.random.fold_in(key_of[14], 71), part)
    w_value = scatter_about(key_of[8], (D, HEADS * HSIZE), D ** -0.5, 0.15625)
    w_out = scatter_about(key_of[9], (HEADS * HSIZE, D), (HEADS * HSIZE) ** -0.5, 0.21875)
    attn_gain = jnp.clip(1.0 + 0.18 * jax.random.normal(key_of[10], (D,), jnp.float32), 0.1, 1.9)
    conv_gain = jnp.clip(1.0 + 0.18 * jax.random.normal(key_of[11], (D,), jnp.float32), 0.1, 1.9)
    conv_kernel = scatter_about(key_of[12], (KSIZE, D), 8 ** -0.5, 2.0, (), jnp.float32)
    conv_scale = jnp.clip(jnp.exp(jax.random.uniform(key_of[13], (D,), jnp.float32, math.log(0.3), math.log(3.0))), 0.3, 3.0)
    return dict(frames=frames, time_starts=time_starts, time_widths=time_widths, freq_starts=freq_starts, freq_widths=freq_widths, lengths=lengths, w_query=w_query, w_key=w_key, w_value=w_value, w_out=w_out, attn_gain=attn_gain, conv_gain=conv_gain, conv_kernel=conv_kernel, conv_scale=conv_scale)


def keep_mask(starts, widths, count):
    places = jnp.arange(count, dtype=jnp.int32)
    inside = (places[None, None, :] >= starts[:, :, None]) & (places[None, None, :] < starts[:, :, None] + widths[:, :, None])
    return 1.0 - jnp.any(inside, axis=1).astype(jnp.float32)

def layer_norm(values, gain):
    values = values.astype(jnp.float32)
    center = lax.optimization_barrier(jnp.mean(values, axis=-1, keepdims=True))
    spread = lax.optimization_barrier(jnp.mean((values - center) ** 2, axis=-1, keepdims=True))
    return (values - center) * lax.rsqrt(spread + 1e-05) * gain

def reference(frames, time_starts, time_widths, freq_starts, freq_widths, lengths, w_query, w_key, w_value, w_out, attn_gain, conv_gain, conv_kernel, conv_scale):
    keep_time = keep_mask(time_starts, time_widths, TIME)
    keep_feat = keep_mask(freq_starts, freq_widths, D)
    masked = (frames.astype(jnp.float32) * keep_time[:, :, None] * keep_feat[:, None, :]).astype(jnp.bfloat16)
    places = jnp.arange(TIME, dtype=jnp.int32)
    valid = (places[None, :] < lengths[:, None]).astype(jnp.float32)
    normed = layer_norm(masked, attn_gain).astype(jnp.bfloat16)
    blocks = TIME // FRAMES
    inner = HEADS * HSIZE

    def one_recording(items):
        rows, source, live, length = items
        query = jnp.dot(rows, w_query, preferred_element_type=jnp.float32).astype(jnp.bfloat16)
        keyed = jnp.dot(rows, w_key, preferred_element_type=jnp.float32).astype(jnp.bfloat16)
        valued = jnp.dot(rows, w_value, preferred_element_type=jnp.float32).astype(jnp.bfloat16)
        query = query.reshape(blocks, FRAMES, HEADS, HSIZE).astype(jnp.float32)
        keyed = keyed.reshape(blocks, FRAMES, HEADS, HSIZE)
        valued = valued.reshape(blocks, FRAMES, HEADS, HSIZE)
        front = jnp.zeros((2, FRAMES, HEADS, HSIZE), jnp.bfloat16)
        keyed = jnp.concatenate([front, keyed], axis=0)
        valued = jnp.concatenate([front, valued], axis=0)
        key_win = jnp.concatenate([keyed[0:blocks], keyed[1:blocks + 1], keyed[2:blocks + 2]], axis=1).astype(jnp.float32)
        value_win = jnp.concatenate([valued[0:blocks], valued[1:blocks + 1], valued[2:blocks + 2]], axis=1).astype(jnp.float32)
        score = jnp.einsum('bqhe,bkhe->bhqk', query, key_win) / jnp.sqrt(jnp.float32(HSIZE))
        block_ids = jnp.arange(blocks, dtype=jnp.int32)
        key_pos = (block_ids[:, None] - 2) * FRAMES + jnp.arange(3 * FRAMES, dtype=jnp.int32)[None, :]
        query_pos = block_ids[:, None] * FRAMES + jnp.arange(FRAMES, dtype=jnp.int32)[None, :]
        allowed = (key_pos[:, None, :] >= 0) & ((key_pos[:, None, :] < length) | (key_pos[:, None, :] == query_pos[:, :, None]))
        score = jnp.where(allowed[:, None, :, :], score, -1e+30)
        top = lax.optimization_barrier(jnp.max(score, axis=-1, keepdims=True))
        weights = jnp.exp(score - top)
        probs = (weights / lax.optimization_barrier(jnp.sum(weights, axis=-1, keepdims=True))).astype(jnp.bfloat16)
        context = jnp.einsum('bhqk,bkhe->bqhe', probs.astype(jnp.float32), value_win)
        context = context.reshape(TIME, inner).astype(jnp.bfloat16)
        mixed = jnp.dot(context, w_out, preferred_element_type=jnp.float32)
        return ((source.astype(jnp.float32) + mixed) * live[:, None]).astype(jnp.bfloat16)
    attended = lax.map(one_recording, (normed, masked, valid, lengths))
    conv_in = layer_norm(attended, conv_gain).astype(jnp.bfloat16)
    padded = jnp.pad(conv_in, ((0, 0), (HALF, HALF), (0, 0))).astype(jnp.float32)
    depth = jnp.zeros((RECS, TIME, D), jnp.float32)
    for step in range(KSIZE):
        depth = depth + conv_kernel[step][None, None, :] * padded[:, step:step + TIME, :]
    result = (attended.astype(jnp.float32) + conv_scale * depth * jax.nn.sigmoid(depth)) * valid[:, :, None]
    return result.astype(jnp.bfloat16)
```

```python
import functools

import jax
import jax.numpy as jnp
from jax import lax
from jax.experimental import pallas as pl
from jax.experimental.pallas import tpu as pltpu
from jax.sharding import PartitionSpec as P

MESH = pl.DeviceIdType.MESH
HSIZE = 64
GROUP = 256
PAD = 16
LANES = 128
AHEAD = 2
LAG = 5


def layer_norm(values, gain):
    center = jnp.mean(values, axis=-1, keepdims=True)
    moved = values - center
    spread = jnp.mean(moved * moved, axis=-1, keepdims=True)
    return moved * lax.rsqrt(spread + 1e-05) * gain


def kernel(
    n,
    time_starts,
    time_widths,
    freq_starts,
    freq_widths,
    lengths,
    frames,
    w_query,
    w_key,
    w_value,
    w_out,
    attn_gain,
    conv_gain,
    conv_kernel,
    conv_scale,
    out,
    masked,
    wq,
    wk,
    wv,
    wo,
    normed,
    query,
    window,
    context,
    attended,
    padded,
    result,
    gains,
    load_sem,
    out_sem,
    z_send,
    z_recv,
    y_send,
    y_recv,
    halo_send,
    halo_recv,
):
    recs, rows, width = masked.shape
    groups = window.shape[0] // recs
    pieces = recs * groups
    wide = width // groups
    me = lax.axis_index("tm")
    odd = lax.rem(me, 2)
    ahead = lax.rem(me + 2, n)
    behind = lax.rem(me + n - 2, n)
    mate = me + 1 - 2 * odd
    other = lax.rem(me + n - 1 + 2 * odd, n)
    after = lax.rem(me + 1, n)
    before = lax.rem(me + n - 1, n)

    loads = []
    for k, (src, dst) in enumerate(
        ((frames, masked), (w_key, wk), (w_value, wv), (w_query, wq), (w_out, wo))
    ):
        copy = pltpu.make_async_copy(src, dst, load_sem.at[k])
        copy.start()
        loads.append(copy)

    barrier = pltpu.get_barrier_semaphore()
    for peer in (behind, mate, other):
        pl.semaphore_signal(barrier, inc=1, device_id={"tm": peer}, device_id_type=MESH)

    local = lax.broadcasted_iota(jnp.int32, (rows, 1), 0)
    place = me * rows + local
    feature = lax.broadcasted_iota(jnp.int32, (1, width), 1)

    def cut(starts, widths, r, places):
        keep = jnp.ones(places.shape, jnp.float32)
        for m in range(starts.shape[0]):
            first = starts[m, r]
            inside = (places >= first) & (places < first + widths[m, r])
            keep = jnp.where(inside, 0.0, keep)
        return keep

    def prepare(r):
        values = masked[r].astype(jnp.float32)
        values = values * cut(time_starts, time_widths, r, place)
        values = values * cut(freq_starts, freq_widths, r, feature)
        masked[r] = values.astype(jnp.bfloat16)
        normed[r] = layer_norm(values, gains[0]).astype(jnp.bfloat16)

    for c in range(width // LANES):
        cols = pl.ds(c * LANES, LANES)
        gains[0, :, cols] = attn_gain[pl.ds(c, 1), :]
        gains[1, :, cols] = conv_gain[pl.ds(c, 1), :]

    def z_copy(k):
        return pltpu.make_async_remote_copy(
            src_ref=window.at[k, pl.ds(2 * rows, rows)],
            dst_ref=window.at[k, pl.ds(0, rows)],
            send_sem=z_send.at[k],
            recv_sem=z_recv.at[k],
            device_id={"tm": ahead},
            device_id_type=MESH,
        )

    def y_copy(k, first):
        return pltpu.make_async_remote_copy(
            src_ref=window.at[k, pl.ds(first, rows)],
            dst_ref=window.at[k, pl.ds(rows, rows)],
            send_sem=y_send.at[k],
            recv_sem=y_recv.at[k],
            device_id={"tm": mate},
            device_id_type=MESH,
        )

    def project(r):
        own = normed[r]
        for g in range(groups):
            cols = pl.ds(g * GROUP, GROUP)
            k = r * groups + g
            window[k, pl.ds(2 * rows, rows), pl.ds(0, GROUP)] = jnp.dot(
                own, wk[:, cols], preferred_element_type=jnp.float32
            ).astype(jnp.bfloat16)
            window[k, pl.ds(2 * rows, rows), pl.ds(GROUP, GROUP)] = jnp.dot(
                own, wv[:, cols], preferred_element_type=jnp.float32
            ).astype(jnp.bfloat16)

    loads[0].wait()
    prepare(0)
    loads[1].wait()
    loads[2].wait()
    project(0)
    pl.semaphore_wait(barrier, 3)
    for k in range(AHEAD):
        z_copy(k).start()

    @pl.when(odd == 0)
    def _():
        y_copy(0, 2 * rows).start()

    def more(r, _):
        prepare(r)
        project(r)
        return 0

    lax.fori_loop(1, recs, more, 0)

    loads[3].wait()

    def ask(r, _):
        own = normed[r]
        for g in range(groups):
            cols = pl.ds(g * GROUP, GROUP)
            asked = jnp.dot(own, wq[:, cols], preferred_element_type=jnp.float32)
            query[r * groups + g] = asked.astype(jnp.bfloat16) * jnp.bfloat16(HSIZE**-0.5)
        return 0

    lax.fori_loop(0, recs, ask, 0)
    loads[4].wait()

    heads = GROUP // HSIZE
    head_of = lax.broadcasted_iota(jnp.int32, (1, GROUP), 1) // HSIZE

    def attend(k):
        r = k // groups
        length = lengths[r]
        keys = window[k, :, pl.ds(0, GROUP)]
        values = window[k, :, pl.ds(GROUP, GROUP)]
        asked = query[k]
        stacked = jnp.concatenate(
            [jnp.where(head_of == h, asked, jnp.zeros_like(asked)) for h in range(heads)], axis=0
        )
        score = lax.dot_general(
            stacked, keys, (((1,), (1,)), ((), ())), preferred_element_type=jnp.float32
        )
        key_pos = (me - 2) * rows + lax.broadcasted_iota(jnp.int32, (rows, 3 * rows), 1)
        allowed = (key_pos >= 0) & ((key_pos < length) | (key_pos == place))
        allowed = jnp.concatenate([allowed] * heads, axis=0)
        score = jnp.where(allowed, score, -1e30)
        top = jnp.max(score, axis=-1, keepdims=True)
        weights = jnp.exp(score - top)
        total = jnp.sum(weights, axis=-1, keepdims=True)
        mixed = jnp.dot(weights.astype(jnp.bfloat16), values, preferred_element_type=jnp.float32)
        mixed = mixed / total
        own = mixed[0:rows]
        for h in range(1, heads):
            own = jnp.where(head_of == h, mixed[h * rows : (h + 1) * rows], own)
        g = lax.rem(k, groups)
        context[r, :, pl.ds(pl.multiple_of(g * GROUP, GROUP), GROUP)] = own.astype(jnp.bfloat16)

    def halo(r, side):
        target = after if side else before
        source = rows if side else PAD
        dest = 0 if side else rows + PAD
        return pltpu.make_async_remote_copy(
            src_ref=padded.at[r, pl.ds(source, PAD)],
            dst_ref=padded.at[r, pl.ds(dest, PAD)],
            send_sem=halo_send.at[r, side],
            recv_sem=halo_recv.at[r, side],
            device_id={"tm": target},
            device_id_type=MESH,
        )

    def finish(r):
        mixed = jnp.dot(context[r], wo[...], preferred_element_type=jnp.float32)
        valid = (place < lengths[r]).astype(jnp.float32)
        held = ((masked[r].astype(jnp.float32) + mixed) * valid).astype(jnp.bfloat16)
        attended[r] = held
        padded[r, pl.ds(PAD, rows)] = layer_norm(
            held.astype(jnp.float32), gains[1]
        ).astype(jnp.bfloat16)
        halo(r, 0).start()
        halo(r, 1).start()

    lead = jnp.where(me > 0, 1.0, 0.0)
    tail = jnp.where(me < n - 1, 1.0, 0.0)
    strips = rows // 8

    def convolve(r, g):
        valid = (place < lengths[r]).astype(jnp.float32)

        def tile(c, _):
            cols = pl.ds(pl.multiple_of(g * wide + c * 128, 128), 128)
            cells = padded[r, :, cols].astype(jnp.float32)
            cells = jnp.concatenate(
                [cells[0:PAD] * lead, cells[PAD : PAD + rows], cells[PAD + rows :] * tail], axis=0
            )
            taps = conv_kernel[:, cols]
            depth = jnp.zeros((rows, 128), jnp.float32)
            for b in range(8):
                part = None
                for a in range(4):
                    j = 8 * a + b
                    if j == 0:
                        continue
                    term = taps[j - 1 : j] * cells[8 * a : 8 * a + rows + 8]
                    part = term if part is None else part + term
                depth = depth + part[b : b + rows]
            held = attended[r, :, cols].astype(jnp.float32)
            gate = depth / (1.0 + jnp.exp(-depth))
            done = (held + conv_scale[pl.ds(g * (wide // LANES) + c, 1), :] * gate) * valid
            result[r, :, cols] = done.astype(jnp.bfloat16)
            return 0

        lax.fori_loop(0, wide // 128, tile, 0)

    def write(r):
        return pltpu.make_async_copy(result.at[r], out.at[r], out_sem.at[r])

    def conv_piece(q):
        r = q // groups
        g = lax.rem(q, groups)

        @pl.when(g == 0)
        def _():
            halo(r, 0).wait_recv()
            halo(r, 1).wait_recv()

        convolve(r, g)

        @pl.when(g == groups - 1)
        def _():
            write(r).start()

    def step(k, _):
        @pl.when(k < pieces)
        def _():
            z_copy(k).wait_recv()

            @pl.when(k + AHEAD < pieces)
            def _():
                z_copy(k + AHEAD).start()

            @pl.when(odd == 1)
            def _():
                y_copy(k, 0).start()

            @pl.when((odd == 0) & (k + 1 < pieces))
            def _():
                y_copy(k + 1, 2 * rows).start()

        @pl.when(k > 0)
        def _():
            p = k - 1
            y_copy(p, 0).wait_recv()
            attend(p)

            @pl.when(lax.rem(p, groups) == groups - 1)
            def _():
                finish(p // groups)

            @pl.when(p >= LAG)
            def _():
                conv_piece(p - LAG)

        return 0

    lax.fori_loop(0, pieces + 1, step, 0)

    def rest(q, _):
        conv_piece(q)
        return 0

    lax.fori_loop(pieces - LAG, pieces, rest, 0)

    def settle(k, _):
        z_copy(k).wait_send()
        y_copy(k, 0).wait_send()
        return 0

    lax.fori_loop(0, pieces, settle, 0)
    for r in range(recs):
        halo(r, 0).wait_send()
        halo(r, 1).wait_send()
        write(r).wait()


def body(
    frames,
    time_starts,
    time_widths,
    freq_starts,
    freq_widths,
    lengths,
    w_query,
    w_key,
    w_value,
    w_out,
    attn_gain,
    conv_gain,
    conv_kernel,
    conv_scale,
):
    n = lax.axis_size("tm")
    recs, rows, width = frames.shape
    inner = w_query.shape[1]
    groups = inner // GROUP
    pieces = recs * groups
    smem = pl.BlockSpec(memory_space=pltpu.SMEM)
    vmem = pl.BlockSpec(memory_space=pltpu.VMEM)
    hbm = pl.BlockSpec(memory_space=pl.ANY)
    dma = pltpu.SemaphoreType.DMA
    return pl.pallas_call(
        functools.partial(kernel, n),
        out_shape=jax.ShapeDtypeStruct((recs, rows, width), jnp.bfloat16),
        in_specs=[smem] * 5 + [hbm] * 5 + [vmem] * 4,
        out_specs=hbm,
        scratch_shapes=[
            pltpu.VMEM((recs, rows, width), jnp.bfloat16),
            pltpu.VMEM((width, inner), jnp.bfloat16),
            pltpu.VMEM((width, inner), jnp.bfloat16),
            pltpu.VMEM((width, inner), jnp.bfloat16),
            pltpu.VMEM((inner, width), jnp.bfloat16),
            pltpu.VMEM((recs, rows, width), jnp.bfloat16),
            pltpu.VMEM((pieces, rows, GROUP), jnp.bfloat16),
            pltpu.VMEM((pieces, 3 * rows, 2 * GROUP), jnp.bfloat16),
            pltpu.VMEM((recs, rows, inner), jnp.bfloat16),
            pltpu.VMEM((recs, rows, width), jnp.bfloat16),
            pltpu.VMEM((recs, rows + 2 * PAD, width), jnp.bfloat16),
            pltpu.VMEM((recs, rows, width), jnp.bfloat16),
            pltpu.VMEM((2, 1, width), jnp.float32),
            dma((5,)),
            dma((recs,)),
            dma((pieces,)),
            dma((pieces,)),
            dma((pieces,)),
            dma((pieces,)),
            dma((recs, 2)),
            dma((recs, 2)),
        ],
        compiler_params=pltpu.CompilerParams(
            collective_id=0, has_side_effects=True, vmem_limit_bytes=56 * 1024 * 1024
        ),
        name="layer",
    )(
        time_starts.T,
        time_widths.T,
        freq_starts.T,
        freq_widths.T,
        lengths,
        frames,
        w_query,
        w_key,
        w_value,
        w_out,
        attn_gain.reshape(width // LANES, LANES),
        conv_gain.reshape(width // LANES, LANES),
        conv_kernel,
        conv_scale.reshape(width // LANES, LANES),
    )


def solution(mesh):
    placed = (
        P("rec", "tm", None),
        P("rec", None),
        P("rec", None),
        P("rec", None),
        P("rec", None),
        P("rec"),
        P(),
        P(),
        P(),
        P(),
        P(),
        P(),
        P(),
        P(),
    )
    return jax.shard_map(
        body, mesh=mesh, in_specs=placed, out_specs=P("rec", "tm", None), check_vma=False
    )
```

```python
import functools

import jax
import jax.numpy as jnp
from jax import lax
from jax.experimental import pallas as pl
from jax.experimental.pallas import tpu as pltpu
from jax.sharding import PartitionSpec as P

MESH = pl.DeviceIdType.MESH
HSIZE = 64
GROUP = 256
PAD = 16
LANES = 128
AHEAD = 3
LAG = 5


def layer_norm(values, gain):
    center = jnp.mean(values, axis=-1, keepdims=True)
    moved = values - center
    spread = jnp.mean(moved * moved, axis=-1, keepdims=True)
    return moved * lax.rsqrt(spread + 1e-05) * gain


def kernel(
    n,
    time_starts,
    time_widths,
    freq_starts,
    freq_widths,
    lengths,
    frames,
    w_query,
    w_key,
    w_value,
    w_out,
    attn_gain,
    conv_gain,
    conv_kernel,
    conv_scale,
    result,
    masked,
    wq,
    wk,
    wv,
    wo,
    normed,
    query,
    window,
    raw,
    context,
    attended,
    padded,
    gains,
    cells,
    load_sem,
    z_send,
    z_recv,
    y_send,
    y_recv,
    halo_send,
    halo_recv,
):
    recs, rows, width = masked.shape
    groups = window.shape[0] // recs
    pieces = recs * groups
    wide = width // groups
    me = lax.axis_index("tm")
    odd = lax.rem(me, 2)
    ahead = jnp.minimum(me + 2, n - 1)
    behind = jnp.maximum(me - 2, 0)
    mate = me + 1 - 2 * odd
    other = jnp.clip(me - 1 + 2 * odd, 0, n - 1)
    after = jnp.minimum(me + 1, n - 1)
    before = jnp.maximum(me - 1, 0)
    sends_z = me < n - 2
    gets_z = me >= 2
    sends_y = me != 1
    gets_y = me != 0
    has_before = me > 0
    has_after = me < n - 1
    has_other = has_before & has_after

    loads = []
    for k, (src, dst) in enumerate(
        ((frames, masked), (w_key, wk), (w_value, wv), (w_query, wq), (w_out, wo))
    ):
        copy = pltpu.make_async_copy(src, dst, load_sem.at[k])
        copy.start()
        loads.append(copy)

    barrier = pltpu.get_barrier_semaphore()

    def greet(peer):
        pl.semaphore_signal(barrier, inc=1, device_id={"tm": peer}, device_id_type=MESH)

    @pl.when(jnp.logical_not(gets_z))
    def _():
        raw[...] = jnp.zeros_like(raw)

        def clear(k, _):
            window[k, pl.ds(0, 2 * rows)] = jnp.zeros((2 * rows, 2 * GROUP), jnp.bfloat16)
            return 0

        lax.fori_loop(0, pieces, clear, 0)

    for present, first in ((has_before, 0), (has_after, rows + PAD)):

        @pl.when(jnp.logical_not(present))
        def _(first=first):
            padded[:, pl.ds(first, PAD)] = jnp.zeros((recs, PAD, width), jnp.bfloat16)

    greet(mate)
    pl.when(gets_z)(lambda: greet(behind))
    pl.when(has_other)(lambda: greet(other))

    local = lax.broadcasted_iota(jnp.int32, (rows, 1), 0)
    place = me * rows + local
    feature = lax.broadcasted_iota(jnp.int32, (1, width), 1)

    def cut(starts, widths, r, places):
        keep = jnp.ones(places.shape, jnp.float32)
        for m in range(starts.shape[0]):
            first = starts[m, r]
            inside = (places >= first) & (places < first + widths[m, r])
            keep = jnp.where(inside, 0.0, keep)
        return keep

    def clean(values, r, places):
        values = values.astype(jnp.float32)
        values = values * cut(time_starts, time_widths, r, places)
        return values * cut(freq_starts, freq_widths, r, feature)

    def prepare(r, _):
        values = clean(masked[r], r, place)
        masked[r] = values.astype(jnp.bfloat16)
        normed[r] = layer_norm(values, gains[0]).astype(jnp.bfloat16)
        return 0

    for c in range(width // LANES):
        cols = pl.ds(c * LANES, LANES)
        gains[0, :, cols] = attn_gain[pl.ds(c, 1), :]
        gains[1, :, cols] = conv_gain[pl.ds(c, 1), :]

    def send(src, dst, sent, got, peer):
        return pltpu.make_async_remote_copy(
            src_ref=src,
            dst_ref=dst,
            send_sem=sent,
            recv_sem=got,
            device_id={"tm": peer},
            device_id_type=MESH,
        )

    def z_copy(k):
        if isinstance(k, int) and k < groups:
            src, dst = frames.at[0, :, pl.ds(k * wide, wide)], raw.at[0, k]
        else:
            src, dst = window.at[k, pl.ds(2 * rows, rows)], window.at[k, pl.ds(0, rows)]
        return send(src, dst, z_send.at[k], z_recv.at[k], ahead)

    def y_copy(k, own):
        if isinstance(k, int) and k < groups:
            src = frames.at[0, :, pl.ds(k * wide, wide)] if own else raw.at[0, k]
            dst = raw.at[1, k]
        else:
            src = window.at[k, pl.ds(2 * rows if own else 0, rows)]
            dst = window.at[k, pl.ds(rows, rows)]
        return send(src, dst, y_send.at[k], y_recv.at[k], mate)

    def relay(k):
        @pl.when(gets_z)
        def _():
            z_copy(k).wait_recv()

        @pl.when((odd == 1) & gets_z)
        def _():
            y_copy(k, False).start()

    def launch(k, z_too=True):
        if z_too:

            @pl.when(sends_z)
            def _():
                z_copy(k).start()

        @pl.when(odd == 0)
        def _():
            y_copy(k, True).start()

    def project(rows_in, r, first):
        for g in range(groups):
            cols = pl.ds(g * GROUP, GROUP)
            k = r * groups + g
            window[k, pl.ds(first, rows), pl.ds(0, GROUP)] = jnp.dot(
                rows_in, wk[:, cols], preferred_element_type=jnp.float32
            ).astype(jnp.bfloat16)
            window[k, pl.ds(first, rows), pl.ds(GROUP, GROUP)] = jnp.dot(
                rows_in, wv[:, cols], preferred_element_type=jnp.float32
            ).astype(jnp.bfloat16)

    def rebuild(side):
        values = jnp.concatenate([raw[side, j] for j in range(groups)], axis=1)
        values = clean(values, 0, place - (2 - side) * rows)
        project(layer_norm(values, gains[0]).astype(jnp.bfloat16), 0, side * rows)

    pl.semaphore_wait(
        barrier, 1 + sends_z.astype(jnp.int32) + has_other.astype(jnp.int32)
    )
    launch(0)
    launch(1)
    loads[0].wait()
    lax.fori_loop(0, recs, prepare, 0)
    loads[1].wait()
    loads[2].wait()
    for r in range(recs):
        project(normed[r], r, 2 * rows)
        relay(r)
        launch(r + 2)

    loads[3].wait()

    def ask(r, _):
        own = normed[r]
        for g in range(groups):
            cols = pl.ds(g * GROUP, GROUP)
            asked = jnp.dot(own, wq[:, cols], preferred_element_type=jnp.float32)
            query[r * groups + g] = asked.astype(jnp.bfloat16) * jnp.bfloat16(HSIZE**-0.5)
        return 0

    lax.fori_loop(0, recs, ask, 0)
    rebuild(0)
    relay(groups)
    launch(groups + 2)

    @pl.when(gets_y)
    def _():
        for j in range(groups):
            y_copy(j, True).wait_recv()

    rebuild(1)
    loads[4].wait()

    heads = GROUP // HSIZE
    head_of = lax.broadcasted_iota(jnp.int32, (1, GROUP), 1) // HSIZE

    def attend(k):
        r = k // groups
        length = lengths[r]
        keys = window[k, :, pl.ds(0, GROUP)]
        values = window[k, :, pl.ds(GROUP, GROUP)]
        asked = query[k]
        stacked = jnp.concatenate(
            [jnp.where(head_of == h, asked, jnp.zeros_like(asked)) for h in range(heads)], axis=0
        )
        score = lax.dot_general(
            stacked, keys, (((1,), (1,)), ((), ())), preferred_element_type=jnp.float32
        )
        key_pos = (me - 2) * rows + lax.broadcasted_iota(jnp.int32, (rows, 3 * rows), 1)
        allowed = (key_pos >= 0) & ((key_pos < length) | (key_pos == place))
        allowed = jnp.concatenate([allowed] * heads, axis=0)
        score = jnp.where(allowed, score, -1e30)
        top = jnp.max(score, axis=-1, keepdims=True)
        weights = jnp.exp(score - top)
        total = jnp.sum(weights, axis=-1, keepdims=True)
        mixed = jnp.dot(weights.astype(jnp.bfloat16), values, preferred_element_type=jnp.float32)
        mixed = mixed / total
        own = mixed[0:rows]
        for h in range(1, heads):
            own = jnp.where(head_of == h, mixed[h * rows : (h + 1) * rows], own)
        g = lax.rem(k, groups)
        context[r, :, pl.ds(pl.multiple_of(g * GROUP, GROUP), GROUP)] = own.astype(jnp.bfloat16)

    def halo(r, side):
        target = after if side else before
        source = rows if side else PAD
        dest = 0 if side else rows + PAD
        return pltpu.make_async_remote_copy(
            src_ref=padded.at[r, pl.ds(source, PAD)],
            dst_ref=padded.at[r, pl.ds(dest, PAD)],
            send_sem=halo_send.at[r, side],
            recv_sem=halo_recv.at[r, side],
            device_id={"tm": target},
            device_id_type=MESH,
        )

    def finish(r):
        mixed = jnp.dot(context[r], wo[...], preferred_element_type=jnp.float32)
        valid = (place < lengths[r]).astype(jnp.float32)
        held = ((masked[r].astype(jnp.float32) + mixed) * valid).astype(jnp.bfloat16)
        attended[r] = held
        padded[r, pl.ds(PAD, rows)] = layer_norm(
            held.astype(jnp.float32), gains[1]
        ).astype(jnp.bfloat16)
        pl.when(has_before)(lambda: halo(r, 0).start())
        pl.when(has_after)(lambda: halo(r, 1).start())

    def convolve(r, g, first, count):
        valid = (place[first : first + count] < lengths[r]).astype(jnp.float32)

        def tile(c, _):
            cols = pl.ds(pl.multiple_of(g * wide + c * LANES, LANES), LANES)
            cells[c, pl.ds(0, count + 2 * PAD)] = padded[r, pl.ds(first, count + 2 * PAD), cols].astype(jnp.float32)
            taps = conv_kernel[:, cols]
            depth = None
            for k in range(taps.shape[0]):
                term = taps[k : k + 1] * cells[c, pl.ds(k + 1, count), :]
                depth = term if depth is None else depth + term
            held = attended[r, pl.ds(first, count), cols].astype(jnp.float32)
            gate = depth / (1.0 + jnp.exp(-depth))
            scale = conv_scale[pl.ds(g * (wide // LANES) + c, 1), :]
            result[r, pl.ds(first, count), cols] = ((held + scale * gate) * valid).astype(
                jnp.bfloat16
            )
            return 0

        lax.fori_loop(0, wide // LANES, tile, 0)

    def meet(r):
        pl.when(has_after)(lambda: halo(r, 0).wait_recv())
        pl.when(has_before)(lambda: halo(r, 1).wait_recv())

    def conv_piece(q):
        r = q // groups
        g = lax.rem(q, groups)
        pl.when(g == 0)(lambda: meet(r))
        convolve(r, g, 0, rows)

    def step(p, _):
        @pl.when((p > 0) & (p + AHEAD < pieces))
        def _():
            relay(p + AHEAD)

            @pl.when(p + AHEAD + 2 < pieces)
            def _():
                launch(p + AHEAD + 2)

        @pl.when(gets_y & (p >= groups))
        def _():
            y_copy(p, True).wait_recv()

        attend(p)

        @pl.when(lax.rem(p, groups) == groups - 1)
        def _():
            finish(p // groups)

        @pl.when(p >= LAG)
        def _():
            conv_piece(p - LAG)

        return 0

    lax.fori_loop(0, pieces, step, 0)

    def rest(q, _):
        conv_piece(q)
        return 0

    lax.fori_loop(pieces - LAG, pieces - groups, rest, 0)
    last = recs - 1

    def inner(g, _):
        convolve(last, g, PAD, rows - 2 * PAD)
        return 0

    lax.fori_loop(0, groups, inner, 0)
    meet(last)

    def edges(g, _):
        convolve(last, g, 0, PAD)
        convolve(last, g, rows - PAD, PAD)
        return 0

    lax.fori_loop(0, groups, edges, 0)

    for k in range(groups):
        pl.when(sends_z)(lambda k=k: z_copy(k).wait_send())
        pl.when(sends_y)(lambda k=k: y_copy(k, True).wait_send())

    def settle(k, _):
        pl.when(sends_z)(lambda: z_copy(k).wait_send())
        pl.when(sends_y)(lambda: y_copy(k, True).wait_send())
        return 0

    lax.fori_loop(groups, pieces, settle, 0)
    for r in range(recs):
        pl.when(has_before)(lambda r=r: halo(r, 0).wait_send())
        pl.when(has_after)(lambda r=r: halo(r, 1).wait_send())


def body(
    frames,
    time_starts,
    time_widths,
    freq_starts,
    freq_widths,
    lengths,
    w_query,
    w_key,
    w_value,
    w_out,
    attn_gain,
    conv_gain,
    conv_kernel,
    conv_scale,
):
    n = lax.axis_size("tm")
    recs, rows, width = frames.shape
    inner = w_query.shape[1]
    groups = inner // GROUP
    pieces = recs * groups
    smem = pl.BlockSpec(memory_space=pltpu.SMEM)
    vmem = pl.BlockSpec(memory_space=pltpu.VMEM)
    hbm = pl.BlockSpec(memory_space=pl.ANY)
    dma = pltpu.SemaphoreType.DMA
    return pl.pallas_call(
        functools.partial(kernel, n),
        out_shape=pltpu.VMEM((recs, rows, width), jnp.bfloat16),
        in_specs=[smem] * 5 + [hbm] * 5 + [vmem] * 4,
        out_specs=vmem,
        scratch_shapes=[
            pltpu.VMEM((recs, rows, width), jnp.bfloat16),
            pltpu.VMEM((width, inner), jnp.bfloat16),
            pltpu.VMEM((width, inner), jnp.bfloat16),
            pltpu.VMEM((width, inner), jnp.bfloat16),
            pltpu.VMEM((inner, width), jnp.bfloat16),
            pltpu.VMEM((recs, rows, width), jnp.bfloat16),
            pltpu.VMEM((pieces, rows, GROUP), jnp.bfloat16),
            pltpu.VMEM((pieces, 3 * rows, 2 * GROUP), jnp.bfloat16),
            pltpu.VMEM((2, groups, rows, width // groups), jnp.bfloat16),
            pltpu.VMEM((recs, rows, inner), jnp.bfloat16),
            pltpu.VMEM((recs, rows, width), jnp.bfloat16),
            pltpu.VMEM((recs, rows + 2 * PAD, width), jnp.bfloat16),
            pltpu.VMEM((2, 1, width), jnp.float32),
            pltpu.VMEM((width // groups // LANES, rows + 2 * PAD, LANES), jnp.float32),
            dma((5,)),
            dma((pieces,)),
            dma((pieces,)),
            dma((pieces,)),
            dma((pieces,)),
            dma((recs, 2)),
            dma((recs, 2)),
        ],
        compiler_params=pltpu.CompilerParams(
            collective_id=0, has_side_effects=True, vmem_limit_bytes=56 * 1024 * 1024
        ),
        name="layer",
    )(
        time_starts.T,
        time_widths.T,
        freq_starts.T,
        freq_widths.T,
        lengths,
        frames,
        w_query,
        w_key,
        w_value,
        w_out,
        attn_gain.reshape(width // LANES, LANES),
        conv_gain.reshape(width // LANES, LANES),
        conv_kernel,
        conv_scale.reshape(width // LANES, LANES),
    )


def solution(mesh):
    placed = (
        P("rec", "tm", None),
        P("rec", None),
        P("rec", None),
        P("rec", None),
        P("rec", None),
        P("rec"),
        P(),
        P(),
        P(),
        P(),
        P(),
        P(),
        P(),
        P(),
    )
    return jax.shard_map(
        body, mesh=mesh, in_specs=placed, out_specs=P("rec", "tm", None), check_vma=False
    )
```

```python
import functools

import jax
import jax.numpy as jnp
from jax import lax
from jax.experimental import pallas as pl
from jax.experimental.pallas import tpu as pltpu
from jax.sharding import PartitionSpec as P

MESH = pl.DeviceIdType.MESH
HSIZE = 64
GROUP = 256
PAD = 16
LANES = 128


def layer_norm(values, gain):
    center = jnp.mean(values, axis=-1, keepdims=True)
    moved = values - center
    spread = jnp.mean(moved * moved, axis=-1, keepdims=True)
    return moved * lax.rsqrt(spread + 1e-05) * gain


def kernel(
    n,
    time_starts,
    time_widths,
    freq_starts,
    freq_widths,
    lengths,
    frames,
    w_query,
    w_key,
    w_value,
    w_out,
    attn_gain,
    conv_gain,
    conv_kernel,
    conv_scale,
    result,
    masked,
    wq,
    wk,
    wv,
    wo,
    query,
    main,
    side,
    raw,
    context,
    returned,
    attended,
    padded,
    gains,
    cells,
    load_sem,
    z_send,
    z_recv,
    y_send,
    y_recv,
    halo_send,
    halo_recv,
):
    recs, rows, width = masked.shape
    groups = main.shape[0]
    wide = width // groups
    heads = GROUP // HSIZE
    me = lax.axis_index("tm")
    odd = lax.rem(me, 2)
    mine, lent, last = odd, 1 - odd, recs - 1
    ahead = jnp.minimum(me + 2, n - 1)
    behind = jnp.maximum(me - 2, 0)
    mate = me + 1 - 2 * odd
    other = jnp.clip(me - 1 + 2 * odd, 0, n - 1)
    after = jnp.minimum(me + 1, n - 1)
    before = jnp.maximum(me - 1, 0)
    sends_z = me < n - 2
    gets_z = me >= 2
    sends_y = me != 1
    gets_y = me != 0
    has_before = me > 0
    has_after = me < n - 1
    has_other = has_before & has_after

    loads = []
    for k, (src, dst) in enumerate(
        ((frames, masked), (w_key, wk), (w_value, wv), (w_query, wq), (w_out, wo))
    ):
        copy = pltpu.make_async_copy(src, dst, load_sem.at[k])
        copy.start()
        loads.append(copy)

    @pl.when(jnp.logical_not(gets_z))
    def _():
        for g in range(groups):
            main[g, pl.ds(0, 2 * rows)] = jnp.zeros((2 * rows, 2 * GROUP), jnp.bfloat16)
            side[g, pl.ds(0, 2 * rows)] = jnp.zeros((2 * rows, 2 * GROUP), jnp.bfloat16)

    for present, first in ((has_before, 0), (has_after, rows + PAD)):

        @pl.when(jnp.logical_not(present))
        def _(first=first):
            padded[:, pl.ds(first, PAD)] = jnp.zeros((recs, PAD, width), jnp.bfloat16)

    barrier = pltpu.get_barrier_semaphore()

    def greet(peer):
        pl.semaphore_signal(barrier, inc=1, device_id={"tm": peer}, device_id_type=MESH)

    greet(mate)
    pl.when(gets_z)(lambda: greet(behind))
    pl.when(has_other)(lambda: greet(other))

    def send(src, dst, sent, got, peer):
        return pltpu.make_async_remote_copy(
            src_ref=src,
            dst_ref=dst,
            send_sem=sent,
            recv_sem=got,
            device_id={"tm": peer},
            device_id_type=MESH,
        )

    def slot(block):
        return pl.ds(pl.multiple_of(block * rows, rows), rows)

    def z_raw(k):
        src = frames.at[last, :, pl.ds(k * wide, wide)]
        return send(src, raw.at[0, k], z_send.at[k], z_recv.at[k], ahead)

    def z_main(g):
        k = groups + g
        src, dst = main.at[g, slot(3 - odd)], main.at[g, slot(1 - odd)]
        return send(src, dst, z_send.at[k], z_recv.at[k], ahead)

    def z_own(g):
        k = 2 * groups + g
        src, dst = main.at[g, slot(2 + odd)], main.at[g, slot(odd)]
        return send(src, dst, z_send.at[k], z_recv.at[k], ahead)

    def y_raw(k):
        src = frames.at[lent, :, pl.ds(k * wide, wide)]
        return send(src, raw.at[1, k], y_send.at[k], y_recv.at[k], mate)

    def y_back(g):
        k = groups + g
        return send(returned.at[g], context.at[mine, g], y_send.at[k], y_recv.at[k], mate)

    def y_side(g, own):
        k = 2 * groups + g
        src = frames.at[last, :, pl.ds(g * wide, wide)] if own else raw.at[0, g]
        return send(src, raw.at[2, g], y_send.at[k], y_recv.at[k], mate)

    def to_z(copy):
        pl.when(sends_z)(lambda: copy.start())

    def left_z(copy):
        pl.when(sends_z)(lambda: copy.wait_send())

    def from_z(copy):
        pl.when(gets_z)(lambda: copy.wait_recv())

    def relay(g):
        from_z(z_raw(g))
        pl.when((odd == 1) & gets_z)(lambda: y_side(g, False).start())

    pl.semaphore_wait(barrier, 1 + sends_z.astype(jnp.int32) + has_other.astype(jnp.int32))
    for k in range(groups):
        to_z(z_raw(k))
        y_raw(k).start()

    local = lax.broadcasted_iota(jnp.int32, (rows, 1), 0)
    place = me * rows + local
    feature = lax.broadcasted_iota(jnp.int32, (1, width), 1)

    def cut(starts, widths, r, places):
        keep = jnp.ones(places.shape, jnp.float32)
        for m in range(starts.shape[0]):
            first = starts[m, r]
            inside = (places >= first) & (places < first + widths[m, r])
            keep = jnp.where(inside, 0.0, keep)
        return keep

    def clean(values, r, places):
        values = values.astype(jnp.float32)
        values = values * cut(time_starts, time_widths, r, places)
        return values * cut(freq_starts, freq_widths, r, feature)

    for c in range(width // LANES):
        cols = pl.ds(c * LANES, LANES)
        gains[0, :, cols] = attn_gain[pl.ds(c, 1), :]
        gains[1, :, cols] = conv_gain[pl.ds(c, 1), :]

    def project(values, window, block, asks):
        normed = layer_norm(values, gains[0]).astype(jnp.bfloat16)

        def column(g, _):
            cols = pl.ds(pl.multiple_of(g * GROUP, GROUP), GROUP)
            window[g, slot(block), pl.ds(0, GROUP)] = jnp.dot(
                normed, wk[:, cols], preferred_element_type=jnp.float32
            ).astype(jnp.bfloat16)
            window[g, slot(block), pl.ds(GROUP, GROUP)] = jnp.dot(
                normed, wv[:, cols], preferred_element_type=jnp.float32
            ).astype(jnp.bfloat16)
            if asks is not None:
                asked = jnp.dot(normed, wq[:, cols], preferred_element_type=jnp.float32)
                query[asks, g] = asked.astype(jnp.bfloat16) * jnp.bfloat16(HSIZE**-0.5)
            return 0

        for g in range(groups):
            column(g, 0)

    def prepare(r):
        values = clean(masked[r], r, place)
        masked[r] = values.astype(jnp.bfloat16)
        return values

    def rebuild(way, r, shift, window, block, asks):
        values = jnp.concatenate([raw[way, k] for k in range(groups)], axis=1)
        project(clean(values, r, place + shift * rows), window, block, asks)

    loads[0].wait()
    held = prepare(last)
    for k in (1, 2, 3):
        loads[k].wait()
    project(held, side, 2, 2)
    project(prepare(mine), main, 2 + odd, 0)
    prepare(lent)
    for k in range(groups):
        left_z(z_raw(k))
        y_raw(k).wait_send()
    for g in range(groups):
        to_z(z_own(g))
        pl.when(odd == 0)(lambda g=g: y_side(g, True).start())
    for g in range(groups):
        relay(g)
    pl.when(gets_z)(lambda: rebuild(0, last, -2, side, 0, None))
    for k in range(groups):
        y_raw(k).wait_recv()
    rebuild(1, mine, 1 - 2 * odd, main, 3 - odd, 1)
    left_z(z_own(0))
    to_z(z_main(0))
    loads[4].wait()

    head_of = lax.broadcasted_iota(jnp.int32, (1, GROUP), 1) // HSIZE

    def attend(keys, values, asked, length, block):
        stacked = jnp.concatenate(
            [jnp.where(head_of == h, asked, jnp.zeros_like(asked)) for h in range(heads)], axis=0
        )
        score = lax.dot_general(
            stacked, keys, (((1,), (1,)), ((), ())), preferred_element_type=jnp.float32
        )
        key_pos = (block - 2) * rows + lax.broadcasted_iota(jnp.int32, (rows, 3 * rows), 1)
        allowed = (key_pos >= 0) & ((key_pos < length) | (key_pos == block * rows + local))
        allowed = jnp.concatenate([allowed] * heads, axis=0)
        score = jnp.where(allowed, score, -1e30)
        top = jnp.max(score, axis=-1, keepdims=True)
        weights = jnp.exp(score - top)
        total = jnp.sum(weights, axis=-1, keepdims=True)
        mixed = jnp.dot(weights.astype(jnp.bfloat16), values, preferred_element_type=jnp.float32)
        mixed = mixed / total
        own = mixed[0:rows]
        for h in range(1, heads):
            own = jnp.where(head_of == h, mixed[h * rows : (h + 1) * rows], own)
        return own.astype(jnp.bfloat16)

    def attend_main(g, which, asks):
        seen = pl.ds(pl.multiple_of(which * rows, rows), 3 * rows)
        return attend(
            main[g, seen, pl.ds(0, GROUP)],
            main[g, seen, pl.ds(GROUP, GROUP)],
            query[asks, g],
            lengths[mine],
            me - odd + which,
        )

    def attend_side(g):
        context[last, g] = attend(
            side[g, :, pl.ds(0, GROUP)],
            side[g, :, pl.ds(GROUP, GROUP)],
            query[2, g],
            lengths[last],
            me,
        )

    def halo(r, way):
        target = after if way else before
        source = rows if way else PAD
        dest = 0 if way else rows + PAD
        return send(
            padded.at[r, pl.ds(source, PAD)],
            padded.at[r, pl.ds(dest, PAD)],
            halo_send.at[r, way],
            halo_recv.at[r, way],
            target,
        )

    def finish(r):
        mixed = jnp.concatenate([context[r, g] for g in range(groups)], axis=1)
        mixed = jnp.dot(mixed, wo[...], preferred_element_type=jnp.float32)
        valid = (place < lengths[r]).astype(jnp.float32)
        held = ((masked[r].astype(jnp.float32) + mixed) * valid).astype(jnp.bfloat16)
        attended[r] = held
        padded[r, pl.ds(PAD, rows)] = layer_norm(
            held.astype(jnp.float32), gains[1]
        ).astype(jnp.bfloat16)
        pl.when(has_before)(lambda: halo(r, 0).start())
        pl.when(has_after)(lambda: halo(r, 1).start())

    def convolve(spans):
        lives = [
            (place[first : first + count] < lengths[r]).astype(jnp.float32)
            for r, first, count in spans
        ]

        def tile(c, carry):
            cols = pl.ds(pl.multiple_of(c * LANES, LANES), LANES)
            taps = conv_kernel[:, cols]
            scale = conv_scale[pl.ds(c, 1), :]
            for i, (r, first, count) in enumerate(spans):
                cells[c, pl.ds(48 * i, count + 2 * PAD)] = padded[
                    r, pl.ds(first, count + 2 * PAD), cols
                ].astype(jnp.float32)
            depths = [None] * len(spans)
            for k in range(taps.shape[0]):
                tap = taps[k : k + 1]
                for i, (_, _, count) in enumerate(spans):
                    term = tap * cells[c, pl.ds(48 * i + k + 1, count), :]
                    depths[i] = term if k == 0 else depths[i] + term
            for i, (r, first, count) in enumerate(spans):
                depth = depths[i]
                held = attended[r, pl.ds(first, count), cols].astype(jnp.float32)
                gate = depth / (1.0 + jnp.exp(-depth))
                done = (held + scale * gate) * lives[i]
                result[r, pl.ds(first, count), cols] = done.astype(jnp.bfloat16)
            return carry

        lax.fori_loop(0, width // LANES, tile, 0)

    def meet(r):
        pl.when(has_after)(lambda: halo(r, 0).wait_recv())
        pl.when(has_before)(lambda: halo(r, 1).wait_recv())

    def inner(r):
        convolve([(r, PAD, rows - 2 * PAD)])

    def edges(*which):
        convolve([(r, first, PAD) for r in which for first in (0, rows - PAD)])

    def pair(g):
        from_z(z_main(g))
        returned[g] = attend_main(g, 1 - odd, 1)
        y_back(g).start()
        context[mine, g] = attend_main(g, odd, 0)

    left_z(z_own(1))
    to_z(z_main(1))

    @pl.when(gets_y)
    def _():
        for g in range(groups):
            y_side(g, True).wait_recv()
        rebuild(2, last, -1, side, 1, None)

    for g in range(groups):
        attend_side(g)
    finish(last)
    left_z(z_own(2))
    left_z(z_main(0))
    to_z(z_main(2))
    for g in range(groups):
        from_z(z_own(g))
    pair(0)
    inner(last)
    pair(1)
    pair(2)
    finish(mine)
    inner(mine)
    for g in range(groups):
        y_back(g).wait_recv()
    finish(lent)
    inner(lent)
    meet(last)
    meet(mine)
    meet(lent)
    edges(last, mine, lent)

    for g in range(groups):
        if g > 0:
            left_z(z_main(g))
        y_back(g).wait_send()
        pl.when(sends_y)(lambda g=g: y_side(g, True).wait_send())
    for r in range(recs):
        pl.when(has_before)(lambda r=r: halo(r, 0).wait_send())
        pl.when(has_after)(lambda r=r: halo(r, 1).wait_send())


def body(
    frames,
    time_starts,
    time_widths,
    freq_starts,
    freq_widths,
    lengths,
    w_query,
    w_key,
    w_value,
    w_out,
    attn_gain,
    conv_gain,
    conv_kernel,
    conv_scale,
):
    n = lax.axis_size("tm")
    recs, rows, width = frames.shape
    inner = w_query.shape[1]
    groups = inner // GROUP
    smem = pl.BlockSpec(memory_space=pltpu.SMEM)
    vmem = pl.BlockSpec(memory_space=pltpu.VMEM)
    hbm = pl.BlockSpec(memory_space=pl.ANY)
    dma = pltpu.SemaphoreType.DMA
    return pl.pallas_call(
        functools.partial(kernel, n),
        out_shape=pltpu.VMEM((recs, rows, width), jnp.bfloat16),
        in_specs=[smem] * 5 + [hbm] * 5 + [vmem] * 4,
        out_specs=vmem,
        scratch_shapes=[
            pltpu.VMEM((recs, rows, width), jnp.bfloat16),
            pltpu.VMEM((width, inner), jnp.bfloat16),
            pltpu.VMEM((width, inner), jnp.bfloat16),
            pltpu.VMEM((width, inner), jnp.bfloat16),
            pltpu.VMEM((inner, width), jnp.bfloat16),
            pltpu.VMEM((3, groups, rows, GROUP), jnp.bfloat16),
            pltpu.VMEM((groups, 4 * rows, 2 * GROUP), jnp.bfloat16),
            pltpu.VMEM((groups, 3 * rows, 2 * GROUP), jnp.bfloat16),
            pltpu.VMEM((3, groups, rows, width // groups), jnp.bfloat16),
            pltpu.VMEM((recs, groups, rows, GROUP), jnp.bfloat16),
            pltpu.VMEM((groups, rows, GROUP), jnp.bfloat16),
            pltpu.VMEM((recs, rows, width), jnp.bfloat16),
            pltpu.VMEM((recs, rows + 2 * PAD, width), jnp.bfloat16),
            pltpu.VMEM((2, 1, width), jnp.float32),
            pltpu.VMEM((width // LANES, 18 * PAD, LANES), jnp.float32),
            dma((5,)),
            dma((3 * groups,)),
            dma((3 * groups,)),
            dma((3 * groups,)),
            dma((3 * groups,)),
            dma((recs, 2)),
            dma((recs, 2)),
        ],
        compiler_params=pltpu.CompilerParams(
            collective_id=0, has_side_effects=True, vmem_limit_bytes=56 * 1024 * 1024
        ),
        name="layer",
    )(
        time_starts.T,
        time_widths.T,
        freq_starts.T,
        freq_widths.T,
        lengths,
        frames,
        w_query,
        w_key,
        w_value,
        w_out,
        attn_gain.reshape(width // LANES, LANES),
        conv_gain.reshape(width // LANES, LANES),
        conv_kernel,
        conv_scale.reshape(width // LANES, LANES),
    )


def solution(mesh):
    placed = (
        P("rec", "tm", None),
        P("rec", None),
        P("rec", None),
        P("rec", None),
        P("rec", None),
        P("rec"),
        P(),
        P(),
        P(),
        P(),
        P(),
        P(),
        P(),
        P(),
    )
    return jax.shard_map(
        body, mesh=mesh, in_specs=placed, out_specs=P("rec", "tm", None), check_vma=False
    )
```

```python
import functools

import jax
import jax.numpy as jnp
from jax import lax
from jax.experimental import pallas as pl
from jax.experimental.pallas import tpu as pltpu
from jax.sharding import PartitionSpec as P

MESH = pl.DeviceIdType.MESH
HSIZE = 64
GROUP = 256
PAD = 16
LANES = 128


def layer_norm(values, gain):
    center = jnp.mean(values, axis=-1, keepdims=True)
    moved = values - center
    spread = jnp.mean(moved * moved, axis=-1, keepdims=True)
    return moved * lax.rsqrt(spread + 1e-05) * gain


def kernel(
    n,
    time_starts,
    time_widths,
    freq_starts,
    freq_widths,
    lengths,
    frames,
    w_query,
    w_key,
    w_value,
    w_out,
    attn_gain,
    conv_gain,
    conv_kernel,
    conv_scale,
    result,
    masked,
    wq,
    wk,
    wv,
    wo,
    query,
    main,
    side,
    raw,
    context,
    returned,
    attended,
    padded,
    gains,
    cells,
    load_sem,
    z_send,
    z_recv,
    y_send,
    y_recv,
    halo_send,
    halo_recv,
):
    recs, rows, width = masked.shape
    groups = main.shape[0]
    wide = width // groups
    heads = GROUP // HSIZE
    me = lax.axis_index("tm")
    odd = lax.rem(me, 2)
    mine, lent, last = odd, 1 - odd, recs - 1
    ahead = jnp.minimum(me + 2, n - 1)
    behind = jnp.maximum(me - 2, 0)
    mate = me + 1 - 2 * odd
    other = jnp.clip(me - 1 + 2 * odd, 0, n - 1)
    after = jnp.minimum(me + 1, n - 1)
    before = jnp.maximum(me - 1, 0)
    sends_z = me < n - 2
    gets_z = me >= 2
    sends_y = me != 1
    gets_y = me != 0
    has_before = me > 0
    has_after = me < n - 1
    has_other = has_before & has_after

    loads = []
    for k, (src, dst) in enumerate(
        ((frames, masked), (w_key, wk), (w_value, wv), (w_query, wq), (w_out, wo))
    ):
        copy = pltpu.make_async_copy(src, dst, load_sem.at[k])
        copy.start()
        loads.append(copy)

    @pl.when(jnp.logical_not(gets_z))
    def _():
        for g in range(groups):
            main[g, pl.ds(0, 2 * rows)] = jnp.zeros((2 * rows, 2 * GROUP), jnp.bfloat16)
            side[g, pl.ds(0, 2 * rows)] = jnp.zeros((2 * rows, 2 * GROUP), jnp.bfloat16)

    for present, first in ((has_before, 0), (has_after, rows + PAD)):

        @pl.when(jnp.logical_not(present))
        def _(first=first):
            padded[:, pl.ds(first, PAD)] = jnp.zeros((recs, PAD, width), jnp.bfloat16)

    barrier = pltpu.get_barrier_semaphore()

    def greet(peer):
        pl.semaphore_signal(barrier, inc=1, device_id={"tm": peer}, device_id_type=MESH)

    greet(mate)
    pl.when(gets_z)(lambda: greet(behind))
    pl.when(has_other)(lambda: greet(other))

    def send(src, dst, sent, got, peer):
        return pltpu.make_async_remote_copy(
            src_ref=src,
            dst_ref=dst,
            send_sem=sent,
            recv_sem=got,
            device_id={"tm": peer},
            device_id_type=MESH,
        )

    def slot(block):
        return pl.ds(pl.multiple_of(block * rows, rows), rows)

    def z_raw(k):
        src = frames.at[last, :, pl.ds(k * wide, wide)]
        return send(src, raw.at[0, k], z_send.at[k], z_recv.at[k], ahead)

    def z_main(g):
        k = groups + g
        src, dst = main.at[g, slot(3 - odd)], main.at[g, slot(1 - odd)]
        return send(src, dst, z_send.at[k], z_recv.at[k], ahead)

    def z_own(g):
        k = 2 * groups + g
        src, dst = main.at[g, slot(2 + odd)], main.at[g, slot(odd)]
        return send(src, dst, z_send.at[k], z_recv.at[k], ahead)

    def y_raw(k):
        src = frames.at[lent, :, pl.ds(k * wide, wide)]
        return send(src, raw.at[1, k], y_send.at[k], y_recv.at[k], mate)

    def y_back(g):
        k = groups + g
        return send(returned.at[g], context.at[mine, g], y_send.at[k], y_recv.at[k], mate)

    def y_side(g, own):
        k = 2 * groups + g
        src = frames.at[last, :, pl.ds(g * wide, wide)] if own else raw.at[0, g]
        return send(src, raw.at[2, g], y_send.at[k], y_recv.at[k], mate)

    def to_z(copy):
        pl.when(sends_z)(lambda: copy.start())

    def left_z(copy):
        pl.when(sends_z)(lambda: copy.wait_send())

    def from_z(copy):
        pl.when(gets_z)(lambda: copy.wait_recv())

    def relay(g):
        from_z(z_raw(g))
        pl.when((odd == 1) & gets_z)(lambda: y_side(g, False).start())

    pl.semaphore_wait(barrier, 1 + sends_z.astype(jnp.int32) + has_other.astype(jnp.int32))
    for k in range(groups):
        to_z(z_raw(k))
        y_raw(k).start()

    local = lax.broadcasted_iota(jnp.int32, (rows, 1), 0)
    place = me * rows + local
    feature = lax.broadcasted_iota(jnp.int32, (1, width), 1)

    def cut(starts, widths, r, places):
        keep = jnp.ones(places.shape, jnp.float32)
        for m in range(starts.shape[0]):
            first = starts[m, r]
            inside = (places >= first) & (places < first + widths[m, r])
            keep = jnp.where(inside, 0.0, keep)
        return keep

    def clean(values, r, places):
        values = values.astype(jnp.float32)
        values = values * cut(time_starts, time_widths, r, places)
        return values * cut(freq_starts, freq_widths, r, feature)

    for c in range(width // LANES):
        cols = pl.ds(c * LANES, LANES)
        gains[0, :, cols] = attn_gain[pl.ds(c, 1), :]
        gains[1, :, cols] = conv_gain[pl.ds(c, 1), :]

    def project(values, window, block, asks):
        normed = layer_norm(values, gains[0]).astype(jnp.bfloat16)

        def column(g, _):
            cols = pl.ds(pl.multiple_of(g * GROUP, GROUP), GROUP)
            window[g, slot(block), pl.ds(0, GROUP)] = jnp.dot(
                normed, wk[:, cols], preferred_element_type=jnp.float32
            ).astype(jnp.bfloat16)
            window[g, slot(block), pl.ds(GROUP, GROUP)] = jnp.dot(
                normed, wv[:, cols], preferred_element_type=jnp.float32
            ).astype(jnp.bfloat16)
            if asks is not None:
                asked = jnp.dot(normed, wq[:, cols], preferred_element_type=jnp.float32)
                query[asks, g] = asked.astype(jnp.bfloat16) * jnp.bfloat16(HSIZE**-0.5)
            return 0

        for g in range(groups):
            column(g, 0)

    def prepare(r):
        values = clean(masked[r], r, place)
        masked[r] = values.astype(jnp.bfloat16)
        return values

    def rebuild(way, r, shift, window, block, asks):
        values = jnp.concatenate([raw[way, k] for k in range(groups)], axis=1)
        project(clean(values, r, place + shift * rows), window, block, asks)

    loads[0].wait()
    held = prepare(last)
    for k in (1, 2, 3):
        loads[k].wait()
    project(held, side, 2, 2)
    project(prepare(mine), main, 2 + odd, 0)
    prepare(lent)
    for k in range(groups):
        left_z(z_raw(k))
        y_raw(k).wait_send()
    for g in range(groups):
        to_z(z_own(g))
        pl.when(odd == 0)(lambda g=g: y_side(g, True).start())
    for g in range(groups):
        relay(g)
    pl.when(gets_z)(lambda: rebuild(0, last, -2, side, 0, None))
    for k in range(groups):
        y_raw(k).wait_recv()
    rebuild(1, mine, 1 - 2 * odd, main, 3 - odd, 1)
    left_z(z_own(0))
    to_z(z_main(0))
    loads[4].wait()

    head_of = lax.broadcasted_iota(jnp.int32, (1, GROUP), 1) // HSIZE

    def attend(keys, values, asked, length, block):
        stacked = jnp.concatenate(
            [jnp.where(head_of == h, asked, jnp.zeros_like(asked)) for h in range(heads)], axis=0
        )
        score = lax.dot_general(
            stacked, keys, (((1,), (1,)), ((), ())), preferred_element_type=jnp.float32
        )
        key_pos = (block - 2) * rows + lax.broadcasted_iota(jnp.int32, (rows, 3 * rows), 1)
        allowed = (key_pos >= 0) & ((key_pos < length) | (key_pos == block * rows + local))
        allowed = jnp.concatenate([allowed] * heads, axis=0)
        score = jnp.where(allowed, score, -1e30)
        top = jnp.max(score, axis=-1, keepdims=True)
        weights = jnp.exp(score - top)
        total = jnp.sum(weights, axis=-1, keepdims=True)
        mixed = jnp.dot(weights.astype(jnp.bfloat16), values, preferred_element_type=jnp.float32)
        mixed = mixed / total
        own = mixed[0:rows]
        for h in range(1, heads):
            own = jnp.where(head_of == h, mixed[h * rows : (h + 1) * rows], own)
        return own.astype(jnp.bfloat16)

    def attend_main(g, which, asks):
        seen = pl.ds(pl.multiple_of(which * rows, rows), 3 * rows)
        return attend(
            main[g, seen, pl.ds(0, GROUP)],
            main[g, seen, pl.ds(GROUP, GROUP)],
            query[asks, g],
            lengths[mine],
            me - odd + which,
        )

    def attend_side(g):
        context[last, g] = attend(
            side[g, :, pl.ds(0, GROUP)],
            side[g, :, pl.ds(GROUP, GROUP)],
            query[2, g],
            lengths[last],
            me,
        )

    def halo(r, way):
        target = after if way else before
        source = rows if way else PAD
        dest = 0 if way else rows + PAD
        return send(
            padded.at[r, pl.ds(source, PAD)],
            padded.at[r, pl.ds(dest, PAD)],
            halo_send.at[r, way],
            halo_recv.at[r, way],
            target,
        )

    def finish(r):
        mixed = jnp.concatenate([context[r, g] for g in range(groups)], axis=1)
        mixed = jnp.dot(mixed, wo[...], preferred_element_type=jnp.float32)
        valid = (place < lengths[r]).astype(jnp.float32)
        held = ((masked[r].astype(jnp.float32) + mixed) * valid).astype(jnp.bfloat16)
        attended[r] = held
        padded[r, pl.ds(PAD, rows)] = layer_norm(
            held.astype(jnp.float32), gains[1]
        ).astype(jnp.bfloat16)
        pl.when(has_before)(lambda: halo(r, 0).start())
        pl.when(has_after)(lambda: halo(r, 1).start())

    def convolve(spans):
        lives = [
            (place[first : first + count] < lengths[r]).astype(jnp.float32)
            for r, first, count in spans
        ]

        def tile(c, carry):
            cols = pl.ds(pl.multiple_of(c * LANES, LANES), LANES)
            taps = conv_kernel[:, cols]
            scale = conv_scale[pl.ds(c, 1), :]
            for i, (r, first, count) in enumerate(spans):
                cells[c, pl.ds(48 * i, count + 2 * PAD)] = padded[
                    r, pl.ds(first, count + 2 * PAD), cols
                ].astype(jnp.float32)
            depths = [None] * len(spans)
            for k in range(taps.shape[0]):
                tap = taps[k : k + 1]
                for i, (_, _, count) in enumerate(spans):
                    term = tap * cells[c, pl.ds(48 * i + k + 1, count), :]
                    depths[i] = term if k == 0 else depths[i] + term
            for i, (r, first, count) in enumerate(spans):
                depth = depths[i]
                held = attended[r, pl.ds(first, count), cols].astype(jnp.float32)
                gate = depth / (1.0 + jnp.exp(-depth))
                done = (held + scale * gate) * lives[i]
                result[r, pl.ds(first, count), cols] = done.astype(jnp.bfloat16)
            return carry

        lax.fori_loop(0, width // LANES, tile, 0)

    def meet(r):
        pl.when(has_after)(lambda: halo(r, 0).wait_recv())
        pl.when(has_before)(lambda: halo(r, 1).wait_recv())

    def inner(r):
        convolve([(r, PAD, rows - 2 * PAD)])

    def edges(*which):
        convolve([(r, first, PAD) for r in which for first in (0, rows - PAD)])

    def pair(g):
        from_z(z_main(g))
        returned[g] = attend_main(g, 1 - odd, 1)
        y_back(g).start()
        context[mine, g] = attend_main(g, odd, 0)

    left_z(z_own(1))
    to_z(z_main(1))

    @pl.when(gets_y)
    def _():
        for g in range(groups):
            y_side(g, True).wait_recv()
        rebuild(2, last, -1, side, 1, None)

    for g in range(groups):
        attend_side(g)
    finish(last)
    left_z(z_own(2))
    left_z(z_main(0))
    to_z(z_main(2))
    inner(last)
    for g in range(groups):
        from_z(z_own(g))
    pair(0)
    pair(1)
    pair(2)
    finish(mine)
    inner(mine)
    for g in range(groups):
        y_back(g).wait_recv()
    finish(lent)
    inner(lent)
    meet(last)
    meet(mine)
    meet(lent)
    edges(last, mine, lent)

    for g in range(groups):
        if g > 0:
            left_z(z_main(g))
        y_back(g).wait_send()
        pl.when(sends_y)(lambda g=g: y_side(g, True).wait_send())
    for r in range(recs):
        pl.when(has_before)(lambda r=r: halo(r, 0).wait_send())
        pl.when(has_after)(lambda r=r: halo(r, 1).wait_send())


def body(
    frames,
    time_starts,
    time_widths,
    freq_starts,
    freq_widths,
    lengths,
    w_query,
    w_key,
    w_value,
    w_out,
    attn_gain,
    conv_gain,
    conv_kernel,
    conv_scale,
):
    n = lax.axis_size("tm")
    recs, rows, width = frames.shape
    inner = w_query.shape[1]
    groups = inner // GROUP
    smem = pl.BlockSpec(memory_space=pltpu.SMEM)
    vmem = pl.BlockSpec(memory_space=pltpu.VMEM)
    hbm = pl.BlockSpec(memory_space=pl.ANY)
    dma = pltpu.SemaphoreType.DMA
    return pl.pallas_call(
        functools.partial(kernel, n),
        out_shape=pltpu.VMEM((recs, rows, width), jnp.bfloat16),
        in_specs=[smem] * 5 + [hbm] * 5 + [vmem] * 4,
        out_specs=vmem,
        scratch_shapes=[
            pltpu.VMEM((recs, rows, width), jnp.bfloat16),
            pltpu.VMEM((width, inner), jnp.bfloat16),
            pltpu.VMEM((width, inner), jnp.bfloat16),
            pltpu.VMEM((width, inner), jnp.bfloat16),
            pltpu.VMEM((inner, width), jnp.bfloat16),
            pltpu.VMEM((3, groups, rows, GROUP), jnp.bfloat16),
            pltpu.VMEM((groups, 4 * rows, 2 * GROUP), jnp.bfloat16),
            pltpu.VMEM((groups, 3 * rows, 2 * GROUP), jnp.bfloat16),
            pltpu.VMEM((3, groups, rows, width // groups), jnp.bfloat16),
            pltpu.VMEM((recs, groups, rows, GROUP), jnp.bfloat16),
            pltpu.VMEM((groups, rows, GROUP), jnp.bfloat16),
            pltpu.VMEM((recs, rows, width), jnp.bfloat16),
            pltpu.VMEM((recs, rows + 2 * PAD, width), jnp.bfloat16),
            pltpu.VMEM((2, 1, width), jnp.float32),
            pltpu.VMEM((width // LANES, 18 * PAD, LANES), jnp.float32),
            dma((5,)),
            dma((3 * groups,)),
            dma((3 * groups,)),
            dma((3 * groups,)),
            dma((3 * groups,)),
            dma((recs, 2)),
            dma((recs, 2)),
        ],
        compiler_params=pltpu.CompilerParams(
            collective_id=0, has_side_effects=True, vmem_limit_bytes=56 * 1024 * 1024
        ),
        name="layer",
    )(
        time_starts.T,
        time_widths.T,
        freq_starts.T,
        freq_widths.T,
        lengths,
        frames,
        w_query,
        w_key,
        w_value,
        w_out,
        attn_gain.reshape(width // LANES, LANES),
        conv_gain.reshape(width // LANES, LANES),
        conv_kernel,
        conv_scale.reshape(width // LANES, LANES),
    )


def solution(mesh):
    placed = (
        P("rec", "tm", None),
        P("rec", None),
        P("rec", None),
        P("rec", None),
        P("rec", None),
        P("rec"),
        P(),
        P(),
        P(),
        P(),
        P(),
        P(),
        P(),
        P(),
    )
    return jax.shard_map(
        body, mesh=mesh, in_specs=placed, out_specs=P("rec", "tm", None), check_vma=False
    )
```

```python
import functools

import jax
import jax.numpy as jnp
from jax import lax
from jax.experimental import pallas as pl
from jax.experimental.pallas import tpu as pltpu
from jax.sharding import PartitionSpec as P

MESH = pl.DeviceIdType.MESH
HSIZE = 64
GROUP = 256
PAD = 16
LANES = 128


def layer_norm(values, gain):
    center = jnp.mean(values, axis=-1, keepdims=True)
    moved = values - center
    spread = jnp.mean(moved * moved, axis=-1, keepdims=True)
    return moved * lax.rsqrt(spread + 1e-05) * gain


def kernel(
    n,
    time_starts,
    time_widths,
    freq_starts,
    freq_widths,
    lengths,
    frames,
    w_query,
    w_key,
    w_value,
    w_out,
    attn_gain,
    conv_gain,
    conv_kernel,
    conv_scale,
    result,
    masked,
    wq,
    wk,
    wv,
    wo,
    query,
    main,
    side,
    raw,
    context,
    returned,
    attended,
    padded,
    gains,
    cells,
    load_sem,
    z_send,
    z_recv,
    y_send,
    y_recv,
    halo_send,
    halo_recv,
):
    recs, rows, width = masked.shape
    groups = main.shape[0]
    wide = width // groups
    heads = GROUP // HSIZE
    me = lax.axis_index("tm")
    odd = lax.rem(me, 2)
    mine, lent, last = odd, 1 - odd, recs - 1
    ahead = jnp.minimum(me + 2, n - 1)
    behind = jnp.maximum(me - 2, 0)
    mate = me + 1 - 2 * odd
    other = jnp.clip(me - 1 + 2 * odd, 0, n - 1)
    after = jnp.minimum(me + 1, n - 1)
    before = jnp.maximum(me - 1, 0)
    sends_z = me < n - 2
    gets_z = me >= 2
    sends_y = me != 1
    gets_y = me != 0
    has_before = me > 0
    has_after = me < n - 1
    has_other = has_before & has_after

    loads = []
    for k, (src, dst) in enumerate(
        ((frames, masked), (w_key, wk), (w_value, wv), (w_query, wq), (w_out, wo))
    ):
        copy = pltpu.make_async_copy(src, dst, load_sem.at[k])
        copy.start()
        loads.append(copy)

    @pl.when(jnp.logical_not(gets_z))
    def _():
        for g in range(groups):
            main[g, pl.ds(0, 2 * rows)] = jnp.zeros((2 * rows, 2 * GROUP), jnp.bfloat16)
            side[g, pl.ds(0, 2 * rows)] = jnp.zeros((2 * rows, 2 * GROUP), jnp.bfloat16)

    for present, first in ((has_before, 0), (has_after, rows + PAD)):

        @pl.when(jnp.logical_not(present))
        def _(first=first):
            padded[:, pl.ds(first, PAD)] = jnp.zeros((recs, PAD, width), jnp.bfloat16)

    barrier = pltpu.get_barrier_semaphore()

    def greet(peer):
        pl.semaphore_signal(barrier, inc=1, device_id={"tm": peer}, device_id_type=MESH)

    greet(mate)
    pl.when(gets_z)(lambda: greet(behind))
    pl.when(has_other)(lambda: greet(other))

    def send(src, dst, sent, got, peer):
        return pltpu.make_async_remote_copy(
            src_ref=src,
            dst_ref=dst,
            send_sem=sent,
            recv_sem=got,
            device_id={"tm": peer},
            device_id_type=MESH,
        )

    def slot(block):
        return pl.ds(pl.multiple_of(block * rows, rows), rows)

    def z_raw(k):
        src = frames.at[last, :, pl.ds(k * wide, wide)]
        return send(src, raw.at[0, k], z_send.at[k], z_recv.at[k], ahead)

    def z_main(g):
        k = groups + g
        src, dst = main.at[g, slot(3 - odd)], main.at[g, slot(1 - odd)]
        return send(src, dst, z_send.at[k], z_recv.at[k], ahead)

    def z_own(g):
        k = 2 * groups + g
        src, dst = main.at[g, slot(2 + odd)], main.at[g, slot(odd)]
        return send(src, dst, z_send.at[k], z_recv.at[k], ahead)

    def y_raw(k):
        src = frames.at[lent, :, pl.ds(k * wide, wide)]
        return send(src, raw.at[1, k], y_send.at[k], y_recv.at[k], mate)

    def y_back(g):
        k = groups + g
        return send(returned.at[g], context.at[mine, g], y_send.at[k], y_recv.at[k], mate)

    def y_side(g, own):
        k = 2 * groups + g
        src = frames.at[last, :, pl.ds(g * wide, wide)] if own else raw.at[0, g]
        return send(src, raw.at[2, g], y_send.at[k], y_recv.at[k], mate)

    def to_z(copy):
        pl.when(sends_z)(lambda: copy.start())

    def left_z(copy):
        pl.when(sends_z)(lambda: copy.wait_send())

    def from_z(copy):
        pl.when(gets_z)(lambda: copy.wait_recv())

    def relay(g):
        from_z(z_raw(g))
        pl.when((odd == 1) & gets_z)(lambda: y_side(g, False).start())

    pl.semaphore_wait(barrier, 1 + sends_z.astype(jnp.int32) + has_other.astype(jnp.int32))
    for k in range(groups):
        to_z(z_raw(k))
        y_raw(k).start()

    local = lax.broadcasted_iota(jnp.int32, (rows, 1), 0)
    place = me * rows + local
    feature = lax.broadcasted_iota(jnp.int32, (1, width), 1)

    def cut(starts, widths, r, places):
        keep = jnp.ones(places.shape, jnp.float32)
        for m in range(starts.shape[0]):
            first = starts[m, r]
            inside = (places >= first) & (places < first + widths[m, r])
            keep = jnp.where(inside, 0.0, keep)
        return keep

    def clean(values, r, places):
        values = values.astype(jnp.float32)
        values = values * cut(time_starts, time_widths, r, places)
        return values * cut(freq_starts, freq_widths, r, feature)

    for c in range(width // LANES):
        cols = pl.ds(c * LANES, LANES)
        gains[0, :, cols] = attn_gain[pl.ds(c, 1), :]
        gains[1, :, cols] = conv_gain[pl.ds(c, 1), :]

    def project(values, window, block, asks):
        normed = layer_norm(values, gains[0]).astype(jnp.bfloat16)

        def column(g, _):
            cols = pl.ds(pl.multiple_of(g * GROUP, GROUP), GROUP)
            window[g, slot(block), pl.ds(0, GROUP)] = jnp.dot(
                normed, wk[:, cols], preferred_element_type=jnp.float32
            ).astype(jnp.bfloat16)
            window[g, slot(block), pl.ds(GROUP, GROUP)] = jnp.dot(
                normed, wv[:, cols], preferred_element_type=jnp.float32
            ).astype(jnp.bfloat16)
            if asks is not None:
                asked = jnp.dot(normed, wq[:, cols], preferred_element_type=jnp.float32)
                query[asks, g] = asked.astype(jnp.bfloat16) * jnp.bfloat16(HSIZE**-0.5)
            return 0

        for g in range(groups):
            column(g, 0)

    def prepare(r):
        values = clean(masked[r], r, place)
        masked[r] = values.astype(jnp.bfloat16)
        return values

    def rebuild(way, r, shift, window, block, asks):
        values = jnp.concatenate([raw[way, k] for k in range(groups)], axis=1)
        project(clean(values, r, place + shift * rows), window, block, asks)

    loads[0].wait()
    held = prepare(last)
    for k in (1, 2, 3):
        loads[k].wait()
    project(held, side, 2, 2)
    project(prepare(mine), main, 2 + odd, 0)
    prepare(lent)
    for k in range(groups):
        left_z(z_raw(k))
        y_raw(k).wait_send()
    for g in range(groups):
        to_z(z_own(g))
        pl.when(odd == 0)(lambda g=g: y_side(g, True).start())
    for g in range(groups):
        relay(g)
    pl.when(gets_z)(lambda: rebuild(0, last, -2, side, 0, None))
    for k in range(groups):
        y_raw(k).wait_recv()
    rebuild(1, mine, 1 - 2 * odd, main, 3 - odd, 1)
    left_z(z_own(0))
    to_z(z_main(0))
    loads[4].wait()

    head_of = lax.broadcasted_iota(jnp.int32, (1, GROUP), 1) // HSIZE

    def attend(keys, values, asked, length, block):
        stacked = jnp.concatenate(
            [jnp.where(head_of == h, asked, jnp.zeros_like(asked)) for h in range(heads)], axis=0
        )
        score = lax.dot_general(
            stacked, keys, (((1,), (1,)), ((), ())), preferred_element_type=jnp.float32
        )
        key_pos = (block - 2) * rows + lax.broadcasted_iota(jnp.int32, (rows, 3 * rows), 1)
        allowed = (key_pos >= 0) & ((key_pos < length) | (key_pos == block * rows + local))
        allowed = jnp.concatenate([allowed] * heads, axis=0)
        score = jnp.where(allowed, score, -1e30)
        top = jnp.max(score, axis=-1, keepdims=True)
        weights = jnp.exp(score - top)
        total = jnp.sum(weights, axis=-1, keepdims=True)
        mixed = jnp.dot(weights.astype(jnp.bfloat16), values, preferred_element_type=jnp.float32)
        mixed = mixed / total
        own = mixed[0:rows]
        for h in range(1, heads):
            own = jnp.where(head_of == h, mixed[h * rows : (h + 1) * rows], own)
        return own.astype(jnp.bfloat16)

    def attend_main(g, which, asks):
        seen = pl.ds(pl.multiple_of(which * rows, rows), 3 * rows)
        return attend(
            main[g, seen, pl.ds(0, GROUP)],
            main[g, seen, pl.ds(GROUP, GROUP)],
            query[asks, g],
            lengths[mine],
            me - odd + which,
        )

    def attend_side(g):
        context[last, g] = attend(
            side[g, :, pl.ds(0, GROUP)],
            side[g, :, pl.ds(GROUP, GROUP)],
            query[2, g],
            lengths[last],
            me,
        )

    def halo(r, way):
        target = after if way else before
        source = rows if way else PAD
        dest = 0 if way else rows + PAD
        return send(
            padded.at[r, pl.ds(source, PAD)],
            padded.at[r, pl.ds(dest, PAD)],
            halo_send.at[r, way],
            halo_recv.at[r, way],
            target,
        )

    def finish(r):
        mixed = jnp.concatenate([context[r, g] for g in range(groups)], axis=1)
        mixed = jnp.dot(mixed, wo[...], preferred_element_type=jnp.float32)
        valid = (place < lengths[r]).astype(jnp.float32)
        held = ((masked[r].astype(jnp.float32) + mixed) * valid).astype(jnp.bfloat16)
        attended[r] = held
        padded[r, pl.ds(PAD, rows)] = layer_norm(
            held.astype(jnp.float32), gains[1]
        ).astype(jnp.bfloat16)
        pl.when(has_before)(lambda: halo(r, 0).start())
        pl.when(has_after)(lambda: halo(r, 1).start())

    def convolve(spans):
        lives = [
            (place[first : first + count] < lengths[r]).astype(jnp.float32)
            for r, first, count in spans
        ]

        def tile(c, carry):
            cols = pl.ds(pl.multiple_of(c * LANES, LANES), LANES)
            taps = conv_kernel[:, cols]
            scale = conv_scale[pl.ds(c, 1), :]
            for i, (r, first, count) in enumerate(spans):
                cells[c, pl.ds(48 * i, count + 2 * PAD)] = padded[
                    r, pl.ds(first, count + 2 * PAD), cols
                ].astype(jnp.float32)
            depths = [None] * len(spans)
            for k in range(taps.shape[0]):
                tap = taps[k : k + 1]
                for i, (_, _, count) in enumerate(spans):
                    term = tap * cells[c, pl.ds(48 * i + k + 1, count), :]
                    depths[i] = term if k == 0 else depths[i] + term
            for i, (r, first, count) in enumerate(spans):
                depth = depths[i]
                held = attended[r, pl.ds(first, count), cols].astype(jnp.float32)
                gate = depth / (1.0 + jnp.exp(-depth))
                done = (held + scale * gate) * lives[i]
                result[r, pl.ds(first, count), cols] = done.astype(jnp.bfloat16)
            return carry

        lax.fori_loop(0, width // LANES, tile, 0)

    def meet(r):
        pl.when(has_after)(lambda: halo(r, 0).wait_recv())
        pl.when(has_before)(lambda: halo(r, 1).wait_recv())

    def inner(r):
        convolve([(r, PAD, rows - 2 * PAD)])

    def edges(*which):
        convolve([(r, first, PAD) for r in which for first in (0, rows - PAD)])

    def pair(g):
        from_z(z_main(g))
        returned[g] = attend_main(g, 1 - odd, 1)
        y_back(g).start()

    left_z(z_own(1))
    to_z(z_main(1))

    @pl.when(gets_y)
    def _():
        for g in range(groups):
            y_side(g, True).wait_recv()
        rebuild(2, last, -1, side, 1, None)

    for g in range(groups):
        attend_side(g)
    finish(last)
    left_z(z_own(2))
    left_z(z_main(0))
    to_z(z_main(2))
    inner(last)
    for g in range(groups):
        from_z(z_own(g))
    pair(0)
    pair(1)
    pair(2)
    for g in range(groups):
        context[mine, g] = attend_main(g, odd, 0)
    finish(mine)
    inner(mine)
    for g in range(groups):
        y_back(g).wait_recv()
    finish(lent)
    inner(lent)
    meet(last)
    meet(mine)
    meet(lent)
    edges(last, mine, lent)

    for g in range(groups):
        if g > 0:
            left_z(z_main(g))
        y_back(g).wait_send()
        pl.when(sends_y)(lambda g=g: y_side(g, True).wait_send())
    for r in range(recs):
        pl.when(has_before)(lambda r=r: halo(r, 0).wait_send())
        pl.when(has_after)(lambda r=r: halo(r, 1).wait_send())


def body(
    frames,
    time_starts,
    time_widths,
    freq_starts,
    freq_widths,
    lengths,
    w_query,
    w_key,
    w_value,
    w_out,
    attn_gain,
    conv_gain,
    conv_kernel,
    conv_scale,
):
    n = lax.axis_size("tm")
    recs, rows, width = frames.shape
    inner = w_query.shape[1]
    groups = inner // GROUP
    smem = pl.BlockSpec(memory_space=pltpu.SMEM)
    vmem = pl.BlockSpec(memory_space=pltpu.VMEM)
    hbm = pl.BlockSpec(memory_space=pl.ANY)
    dma = pltpu.SemaphoreType.DMA
    return pl.pallas_call(
        functools.partial(kernel, n),
        out_shape=pltpu.VMEM((recs, rows, width), jnp.bfloat16),
        in_specs=[smem] * 5 + [hbm] * 5 + [vmem] * 4,
        out_specs=vmem,
        scratch_shapes=[
            pltpu.VMEM((recs, rows, width), jnp.bfloat16),
            pltpu.VMEM((width, inner), jnp.bfloat16),
            pltpu.VMEM((width, inner), jnp.bfloat16),
            pltpu.VMEM((width, inner), jnp.bfloat16),
            pltpu.VMEM((inner, width), jnp.bfloat16),
            pltpu.VMEM((3, groups, rows, GROUP), jnp.bfloat16),
            pltpu.VMEM((groups, 4 * rows, 2 * GROUP), jnp.bfloat16),
            pltpu.VMEM((groups, 3 * rows, 2 * GROUP), jnp.bfloat16),
            pltpu.VMEM((3, groups, rows, width // groups), jnp.bfloat16),
            pltpu.VMEM((recs, groups, rows, GROUP), jnp.bfloat16),
            pltpu.VMEM((groups, rows, GROUP), jnp.bfloat16),
            pltpu.VMEM((recs, rows, width), jnp.bfloat16),
            pltpu.VMEM((recs, rows + 2 * PAD, width), jnp.bfloat16),
            pltpu.VMEM((2, 1, width), jnp.float32),
            pltpu.VMEM((width // LANES, 18 * PAD, LANES), jnp.float32),
            dma((5,)),
            dma((3 * groups,)),
            dma((3 * groups,)),
            dma((3 * groups,)),
            dma((3 * groups,)),
            dma((recs, 2)),
            dma((recs, 2)),
        ],
        compiler_params=pltpu.CompilerParams(
            collective_id=0, has_side_effects=True, vmem_limit_bytes=56 * 1024 * 1024
        ),
        name="layer",
    )(
        time_starts.T,
        time_widths.T,
        freq_starts.T,
        freq_widths.T,
        lengths,
        frames,
        w_query,
        w_key,
        w_value,
        w_out,
        attn_gain.reshape(width // LANES, LANES),
        conv_gain.reshape(width // LANES, LANES),
        conv_kernel,
        conv_scale.reshape(width // LANES, LANES),
    )


def solution(mesh):
    placed = (
        P("rec", "tm", None),
        P("rec", None),
        P("rec", None),
        P("rec", None),
        P("rec", None),
        P("rec"),
        P(),
        P(),
        P(),
        P(),
        P(),
        P(),
        P(),
        P(),
    )
    return jax.shard_map(
        body, mesh=mesh, in_specs=placed, out_specs=P("rec", "tm", None), check_vma=False
    )
```
